1024 devices in a mesh: fsdp: 32 (over z), head: 8 (over x, core), rep: 4 (over y).
Axes of the slice: x: 4, y: 4, z: 32, core: 2. Of those that a mesh axis runs over, the one named last changes fastest.
Arguments:
- expert_master: float32 [32, 7168, 2048], P(None, ('rep', 'fsdp'), 'head'), may hold values from -0.0625 to 0.0625
- placement: int32 [32], replicated, may hold values from 0 to 31, as said below
- hidden_rows: bfloat16 [512, 7168], P(None, 'rep'), may hold values from -6 to 6
- routes: int32 [512, 8], replicated, may hold values from 0 to 31, all different within a row
- route_weight: float32 [512, 8], replicated, may hold values from 0.1 to 1
- att_master: float32 [512, 64, 256], P(('fsdp', 'head')), may hold values from -0.5 to 0.5
- query_nope: bfloat16 [4, 512, 64, 128], P(None, ('fsdp', 'rep'), 'head'), may hold values from -6 to 6
- query_rope: bfloat16 [4, 512, 64, 64], P(None, ('fsdp', 'rep'), 'head'), may hold values from -250 to 250
- cache_latent: bfloat16 [512, 512, 576], P(('fsdp', 'rep')), may hold values from -4.1 to 4.1
- cache_len: int32 [512], P(('fsdp', 'rep')), may hold values from 2 to 512, as said below
- new_latent: bfloat16 [4, 512, 576], P(None, ('fsdp', 'rep')), may hold values from -4 to 4
Outputs:
- expert_hidden: bfloat16 [64, 512, 2048], P('fsdp', 'rep', 'head')
- attention_out: bfloat16 [4, 512, 8192], P(None, ('fsdp', 'rep'), 'head')
The draws below stay inside these ranges and needn't reach their ends.
Inputs may be any that keep to these rules, and one draw needn't show every extreme that they name: `placement`: each owner holds at most 2 experts, and some owner holds exactly 2. `cache_len`: row 0 uses every position.
All inputs are finite; a program needn't handle non-finite values.
Results may differ from the reference program's by a relative error of at most 0.0081.
Values may be sent and summed in bfloat16 or wider, within the bound.
A program may use at most 64 MiB of HBM per device.

```python
import math
import jax
import jax.numpy as jnp
from jax import lax

D = 7168
FF = 2048
HEADS = 64
LAT = 512
HDIM = 128
ROPE = 64
SLOTS = 2
STEPS = 4
CACHE = 512
E = 32
TOP = 8
ROWS = 512
N_FSDP = 32


def shared_rope(key):
    return jnp.clip(jax.random.normal(key, (ROWS, CACHE, ROPE), jnp.float32), -4.0, 4.0)


def draw_cache_latent(key, part):
    rope = shared_rope(key)
    key = jax.random.fold_in(key, 11)
    latent = jnp.clip(jax.random.normal(key, (ROWS, CACHE, LAT), jnp.float32), -4.0, 4.0)
    return jnp.concatenate([latent, rope], axis=2).astype(jnp.bfloat16)


def draw_query_rope(key, part):
    key = jax.random.fold_in(key, 12)
    first = jax.random.fold_in(key, 0)
    values = jnp.clip(jax.random.normal(first, (STEPS, ROWS, HEADS, ROPE), jnp.float32), -4.0, 4.0)
    return values.astype(jnp.bfloat16)


def draw_cache_len(key, part):
    key = jax.random.fold_in(key, 13)
    lengths = jax.random.randint(key, (ROWS,), 2, CACHE + 1)
    return lengths.at[0].set(CACHE).astype(jnp.int32)


def draw_placement(key, part):
    key = jax.random.fold_in(key, 14)
    first, second = jax.random.split(key)
    seats = jax.random.permutation(first, SLOTS * N_FSDP)
    full_owner = seats[0] // SLOTS
    order = jnp.argsort((seats // SLOTS == full_owner).astype(jnp.int32), stable=True)
    others = seats[order]
    owners = jnp.concatenate([jnp.full((SLOTS,), full_owner, jnp.int32), (others[:E - SLOTS] // SLOTS).astype(jnp.int32)])
    return jax.random.permutation(second, owners).astype(jnp.int32)


def steps_of(key, extent, shards, low, top_value):
    factor_of, own = 1.0, jax.random.fold_in(key, 6)
    for position, parts in shards:
        steps = jnp.exp(jax.random.uniform(jax.random.fold_in(own, position), (parts,), jnp.float32, low / len(shards), top_value / len(shards)))
        factor_of = factor_of * jnp.repeat(steps, extent[position] // parts).reshape([-1 if axis == position else 1 for axis in range(len(extent))])
    return factor_of


def different_ones(key, rows, amount, top, lift):
    ranking = jax.random.permutation(jax.random.fold_in(key, 1), amount)
    boost = ranking
    for power in range(3):
        boost = boost * boost // amount
    boost = boost * lift // amount
    tickets = jax.random.randint(jax.random.fold_in(key, 2), (rows, amount), 0, 4096) + boost
    holders = jax.random.permutation(jax.random.fold_in(key, 3), rows)[jnp.arange(amount) % rows]
    tickets = jnp.where(jnp.arange(rows)[:, None] == holders[None, :], 1 << 14, tickets)
    merit = tickets * amount + jnp.arange(amount)
    return lax.top_k(merit.astype(jnp.int32), top)[1].astype(jnp.int32)


def normal_values(key, extent, spread, limit, cuts=(), kind=jnp.bfloat16):
    factor_of = steps_of(key, extent, cuts, -0.22, 0.18) if cuts else 1.0
    values = jax.random.normal(key, extent, jnp.float32) * spread * factor_of
    return jnp.minimum(jnp.maximum(values, -limit), limit).astype(kind)


def setup_inputs(seed: int = 0) -> dict:
    keys = jax.random.split(jax.random.key(seed), 12)
    return {
        "expert_master": normal_values(keys[0], (E, D, FF), D ** -0.5, 0.0625, ((1, 128), (2, 8)), jnp.float32),
        "placement": draw_placement(jax.random.fold_in(keys[11], 71), 0),
        "hidden_rows": normal_values(keys[2], (ROWS, D), 1.0, 6.0, ((1, 4),)),
        "routes": different_ones(keys[3], ROWS, E, TOP, 4096),
        "route_weight": jnp.clip(jax.random.uniform(keys[4], (ROWS, TOP), jnp.float32, 0.1, 1.0), 0.1, 1.0),
        "att_master": normal_values(keys[5], (LAT, HEADS, 2 * HDIM), HDIM ** -0.5, 0.5, ((0, 256),), jnp.float32),
        "query_nope": normal_values(keys[6], (STEPS, ROWS, HEADS, HDIM), 1.0, 6.0, ((1, 128), (2, 8))),
        "query_rope": draw_query_rope(jax.random.fold_in(keys[11], 71), 0),
        "cache_latent": draw_cache_latent(jax.random.fold_in(keys[11], 71), 0),
        "cache_len": draw_cache_len(jax.random.fold_in(keys[11], 71), 0),
        "new_latent": normal_values(keys[10], (STEPS, ROWS, LAT + ROPE), 1.0, 4.0, ((1, 128),)),
    }


def attend(maps, query_nope, query_rope, cache_latent, cache_len, new_latent):
    f32 = jnp.float32
    key_map = maps[:, :, :HDIM].astype(f32)
    value_map = maps[:, :, HDIM:].astype(f32)
    q_latent = jnp.einsum('trhd,lhd->trhl', query_nope.astype(f32), key_map).astype(jnp.bfloat16)
    query_full = jnp.concatenate([q_latent, query_rope], axis=3).astype(f32)
    scale = 1.0 / math.sqrt(HDIM + ROPE)
    cache_wide = cache_latent.astype(f32)
    new_wide = new_latent.astype(f32)
    old_scores = jnp.einsum('trhc,rjc->trhj', query_full, cache_wide) * scale
    new_scores = jnp.einsum('trhc,urc->trhu', query_full, new_wide) * scale
    positions = jnp.arange(cache_latent.shape[1], dtype=jnp.int32)
    live = positions[None, :] < cache_len[:, None]
    old_scores = jnp.where(live[None, :, None, :], old_scores, -1e+30)
    step_ids = jnp.arange(new_latent.shape[0], dtype=jnp.int32)
    causal = step_ids[None, :] <= step_ids[:, None]
    new_scores = jnp.where(causal[:, None, None, :], new_scores, -1e+30)
    top = jnp.maximum(lax.optimization_barrier(jnp.max(old_scores, axis=3)), lax.optimization_barrier(jnp.max(new_scores, axis=3)))
    old_exp = jnp.exp(old_scores - top[..., None])
    new_exp = jnp.exp(new_scores - top[..., None])
    total = lax.optimization_barrier(jnp.sum(old_exp, axis=3)) + lax.optimization_barrier(jnp.sum(new_exp, axis=3))
    old_probs = (old_exp / total[..., None]).astype(jnp.bfloat16).astype(f32)
    new_probs = (new_exp / total[..., None]).astype(jnp.bfloat16).astype(f32)
    latent_full = jnp.einsum('trhj,rjc->trhc', old_probs, cache_wide) + jnp.einsum('trhu,urc->trhc', new_probs, new_wide)
    latent_out = latent_full[..., :LAT].astype(jnp.bfloat16).astype(f32)
    attention = jnp.einsum('trhl,lhv->trhv', latent_out, value_map).astype(jnp.bfloat16)
    return attention.reshape(attention.shape[0], attention.shape[1], attention.shape[2] * attention.shape[3])

def reference(expert_master, placement, hidden_rows, routes, route_weight, att_master, query_nope, query_rope, cache_latent, cache_len, new_latent):
    expert_ids = jnp.arange(E, dtype=jnp.int32)
    same = placement[:, None] == placement[None, :]
    earlier = expert_ids[None, :] < expert_ids[:, None]
    slot = lax.optimization_barrier(jnp.sum((same & earlier).astype(jnp.int32), axis=1)).astype(jnp.int32)
    target = (placement * SLOTS + slot).astype(jnp.int32)

    def one_expert(index):
        moved = expert_master[index].astype(jnp.bfloat16)
        preact = jnp.dot(hidden_rows, moved, preferred_element_type=jnp.float32)
        gate = lax.optimization_barrier(jnp.sum(jnp.where(routes == index, route_weight, jnp.zeros_like(route_weight)), axis=1))
        return (jax.nn.silu(preact) * gate[:, None]).astype(jnp.bfloat16)
    per_expert = lax.map(one_expert, expert_ids)
    expert_hidden = jnp.zeros((N_FSDP * SLOTS, ROWS, FF), jnp.bfloat16).at[target].set(per_expert)
    maps = att_master.astype(jnp.bfloat16)
    block = math.gcd(ROWS, 32)
    count = ROWS // block
    q_nope_b = jnp.swapaxes(query_nope.reshape(STEPS, count, block, HEADS, HDIM), 0, 1)
    q_rope_b = jnp.swapaxes(query_rope.reshape(STEPS, count, block, HEADS, ROPE), 0, 1)
    cache_b = cache_latent.reshape(count, block, CACHE, LAT + ROPE)
    len_b = cache_len.reshape(count, block)
    new_b = jnp.swapaxes(new_latent.reshape(STEPS, count, block, LAT + ROPE), 0, 1)

    def one_block(pieces):
        return attend(maps, pieces[0], pieces[1], pieces[2], pieces[3], pieces[4])
    outs = lax.map(one_block, (q_nope_b, q_rope_b, cache_b, len_b, new_b))
    attention_out = jnp.swapaxes(outs, 0, 1).reshape(STEPS, ROWS, HEADS * HDIM)
    return (expert_hidden, attention_out)
```

```python
import functools
import math

import jax
import jax.numpy as jnp
from jax import lax
from jax.experimental import pallas as pl
from jax.experimental.pallas import tpu as pltpu
from jax.sharding import PartitionSpec as P

MESH = pl.DeviceIdType.MESH
SLOTS = 2
GROUP = 8
F32 = jnp.float32
BF16 = jnp.bfloat16
SPREADS = (3.2, None)


def capacities(n, spread):
    caps = [0]
    for length in range(1, n // 2 + 1):
        cap = 2 * length
        if spread is not None:
            drift = math.sqrt(2 * length * 0.25 * (2 * n - 2 * length) / (2 * n - 1))
            cap = min(cap, int(length + spread * drift))
        caps.append(max(cap, caps[-1], 2))
    return tuple(caps)


class Kind:
    def __init__(self, index, sign, part, reach, caps):
        self.index, self.sign, self.part, self.reach, self.caps = index, sign, part, reach, caps

    def sent(self, hop):
        return self.caps[self.reach - hop + 1]

    def pieces(self, hop):
        if hop < 1 or hop > self.reach:
            return []
        top = self.sent(hop)
        return [(low, min(low + GROUP, top)) for low in range(0, top, GROUP)]


def kinds_of(n, caps):
    half = n // 2
    return (
        Kind(0, 1, 0, half, caps),
        Kind(1, -1, 0, half - 1, caps),
        Kind(2, 1, 1, half - 1, caps),
        Kind(3, -1, 1, half, caps),
    )


def body(
    n,
    heads,
    reps,
    caps,
    tbl,
    lens,
    master_hbm,
    x_hbm,
    gate,
    att,
    qn,
    qr,
    cache_hbm,
    new,
    eh_out,
    at_out,
    *refs,
):
    z, h, y = lax.axis_index("fsdp"), lax.axis_index("head"), lax.axis_index("rep")
    kinds = kinds_of(n, caps)
    bufs = []
    for kind in kinds:
        bufs.append(refs[: kind.reach + 1])
        refs = refs[kind.reach + 1 :]
    (
        master,
        x,
        cache,
        wide_x,
        spread,
        weights,
        landed,
        maps,
        qlat,
        probs,
        latent,
        rs_out,
        rs_in,
        send_sem,
        recv_sem,
        head_send,
        head_recv,
        map_send,
        map_recv,
        y_send,
        y_recv,
        rs_send,
        rs_recv,
        load_sem,
    ) = refs
    half = n // 2
    zn = z + n
    rows = master.shape[1]
    units = master.shape[2]
    lanes = units // 2
    head_rows = rows * 4 // 7
    tail_rows = rows - head_rows
    pad_rows = wide_x.shape[1] // n
    share = x.shape[0] // reps
    local_heads, lat = maps.shape[0], maps.shape[1]
    hdim = maps.shape[2] // 2
    block = lat // n
    z_to = {1: lax.rem(z + 1, n), -1: lax.rem(z + n - 1, n)}
    y_to = {1: lax.rem(y + 1, reps), -1: lax.rem(y + reps - 1, reps)}
    y_far = lax.rem(y + 2, reps)

    loads = [
        pltpu.make_async_copy(master_hbm, master, load_sem.at[0]),
        pltpu.make_async_copy(x_hbm, x, load_sem.at[1]),
        pltpu.make_async_copy(cache_hbm, cache, load_sem.at[2]),
    ]
    for load in loads:
        load.start()

    barrier = pltpu.get_barrier_semaphore()
    for sign in (1, -1):
        pl.semaphore_signal(barrier, inc=1, device_id={"fsdp": z_to[sign]}, device_id_type=MESH)
        pl.semaphore_signal(barrier, inc=1, device_id={"rep": y_to[sign]}, device_id_type=MESH)
    for step in range(1, heads):
        pl.semaphore_signal(
            barrier, inc=1, device_id={"head": lax.rem(h + step, heads)}, device_id_type=MESH
        )
    pl.semaphore_wait(barrier, 4 + heads - 1)

    head_copies = []
    for step in range(1, heads):
        to = lax.rem(h + step, heads)
        copy = pltpu.make_async_remote_copy(
            src_ref=att.at[to],
            dst_ref=landed.at[h],
            send_sem=head_send.at[step],
            recv_sem=head_recv.at[h],
            device_id={"head": to},
            device_id_type=MESH,
        )
        copy.start()
        head_copies.append(copy)

    def head_arrival(step):
        source = lax.rem(h + step, heads)
        return pltpu.make_async_remote_copy(
            src_ref=att.at[source],
            dst_ref=landed.at[source],
            send_sem=head_send.at[step],
            recv_sem=head_recv.at[source],
            device_id={"head": source},
            device_id_type=MESH,
        )

    def map_block(sign, hop):
        owner = lax.rem(zn - sign * hop, n)
        return maps.at[pl.ds(2 * y, 2), pl.ds(pl.multiple_of(owner * block, block), block), :]

    def map_copy(sign, hop):
        index = half * (sign < 0) + hop - 1
        ref = map_block(sign, hop - 1)
        return pltpu.make_async_remote_copy(
            src_ref=ref,
            dst_ref=ref,
            send_sem=map_send.at[index],
            recv_sem=map_recv.at[index],
            device_id={"fsdp": z_to[sign]},
            device_id_type=MESH,
        )

    def map_arrival(sign, hop):
        index = half * (sign < 0) + hop - 1
        ref = map_block(sign, hop)
        return pltpu.make_async_remote_copy(
            src_ref=ref,
            dst_ref=ref,
            send_sem=map_send.at[index],
            recv_sem=map_recv.at[index],
            device_id={"fsdp": z_to[sign]},
            device_id_type=MESH,
        )

    def y_copy(index, sign, low, size):
        ref = maps.at[pl.ds(low, size)]
        return pltpu.make_async_remote_copy(
            src_ref=ref,
            dst_ref=ref,
            send_sem=y_send.at[index],
            recv_sem=y_recv.at[index],
            device_id={"rep": y_to[sign]},
            device_id_type=MESH,
        )

    open_sends = []

    def attention():
        for step in range(1, heads):
            head_arrival(step).wait_recv()
        landed[h] = att[h]
        flat = landed[...].reshape(heads * att.shape[1], att.shape[2]).astype(BF16)
        per = att.shape[1]
        for hq in range(2):
            for side in range(2):
                row = lax.broadcasted_iota(jnp.int32, (block, heads * per), 0)
                col = lax.broadcasted_iota(jnp.int32, (block, heads * per), 1)
                want = (row >> 1) * per + hq * 4 + (row & 1) * 2 + side
                pick = jnp.where(col == want, 1.0, 0.0).astype(BF16)
                piece = jnp.dot(pick, flat, preferred_element_type=F32).astype(BF16)
                maps[
                    2 * y + hq,
                    pl.ds(pl.multiple_of(z * block, block), block),
                    side * hdim : (side + 1) * hdim,
                ] = piece
        for hop in range(1, half + 2):
            for sign in (1, -1):
                top = half if sign > 0 else half - 1
                if 2 <= hop <= top + 1:
                    map_arrival(sign, hop - 1).wait_recv()
                if hop <= top:
                    copy = map_copy(sign, hop)
                    copy.start()
                    open_sends.append(copy)
            yield
        first = [y_copy(0, 1, 2 * y, 2), y_copy(1, -1, 2 * y, 2)]
        for copy in first:
            copy.start()
            open_sends.append(copy)
        for _ in range(5):
            yield
        y_copy(0, 1, 2 * y_to[-1], 2).wait_recv()
        y_copy(1, -1, 2 * y_to[1], 2).wait_recv()
        second = [y_copy(2, 1, 2 * y_to[-1], 1), y_copy(3, -1, 2 * y_to[1] + 1, 1)]
        for copy in second:
            copy.start()
            open_sends.append(copy)
        for _ in range(3):
            yield
        y_copy(2, 1, 2 * y_far, 1).wait_recv()
        y_copy(3, -1, 2 * y_far + 1, 1).wait_recv()
        loads[2].wait()
        yield
        group = qn.shape[0]
        contract = (((1,), (1,)), ((), ()))
        for head in range(local_heads):
            q = qn[:, head * hdim : (head + 1) * hdim]
            qlat[head * group : (head + 1) * group, :] = lax.dot_general(
                q, maps[head, :, :hdim], contract, preferred_element_type=F32
            ).astype(BF16)
        yield
        total_rows = local_heads * group
        count, slots = cache.shape[0], cache.shape[2]
        scale = 1.0 / math.sqrt(hdim + qr.shape[1])
        row = lax.broadcasted_iota(jnp.int32, (total_rows, slots), 0) & (count - 1)
        col = lax.broadcasted_iota(jnp.int32, (total_rows, slots), 1)
        score = jnp.full((total_rows, slots), -1e30, F32)
        for r in range(count):
            part = jnp.dot(qlat[...], cache[r, :lat, :], preferred_element_type=F32) + jnp.dot(
                qr[...], cache[r, lat:, :], preferred_element_type=F32
            )
            score = jnp.where((row == r) & (col < lens[r]), part * scale, score)
        fresh = lax.dot_general(
            qlat[...], new[:, :lat], contract, preferred_element_type=F32
        ) + lax.dot_general(qr[...], new[:, lat:], contract, preferred_element_type=F32)
        nrow = lax.broadcasted_iota(jnp.int32, fresh.shape, 0)
        ncol = lax.broadcasted_iota(jnp.int32, fresh.shape, 1)
        shift = count.bit_length() - 1
        same = (nrow & (count - 1)) == (ncol & (count - 1))
        step_of = (nrow >> shift) & (group // count - 1)
        fresh = jnp.where(same & ((ncol >> shift) <= step_of), fresh * scale, -1e30)
        top = jnp.maximum(
            jnp.max(score, axis=1, keepdims=True), jnp.max(fresh, axis=1, keepdims=True)
        )
        old_exp = jnp.exp(score - top)
        new_exp = jnp.exp(fresh - top)
        total = jnp.sum(old_exp, axis=1, keepdims=True) + jnp.sum(new_exp, axis=1, keepdims=True)
        probs[...] = old_exp / total
        new_probs = (new_exp / total).astype(BF16)
        latent[...] = jnp.dot(new_probs, new[:, :lat], preferred_element_type=F32)
        yield
        for r in range(count):
            mine = jnp.where(row == r, probs[...], 0.0).astype(BF16)
            latent[...] += lax.dot_general(
                mine, cache[r, :lat, :], contract, preferred_element_type=F32
            )
        yield
        for head in range(local_heads):
            lh = latent[head * group : (head + 1) * group, :].astype(BF16)
            at_out[:, head * hdim : (head + 1) * hdim] = jnp.dot(
                lh, maps[head, :, hdim:], preferred_element_type=F32
            ).astype(BF16)

    def widen():
        for slot in range(SLOTS):
            rank = jnp.clip(tbl[0, zn] + slot, 0, tbl.shape[1] - 1)
            expert = jnp.clip(tbl[1, rank], 0, master.shape[0] - 1)
            weights[slot, pl.ds(pl.multiple_of(z * pad_rows, pad_rows), rows), :] = master[
                expert
            ].astype(BF16)
        loads[1].wait()
        yield
        row = lax.broadcasted_iota(jnp.int32, spread.shape, 0)
        col = lax.broadcasted_iota(jnp.int32, spread.shape, 1)
        inside = col & (pad_rows - 1)
        source = col >> (pad_rows.bit_length() - 1)
        spread[...] = jnp.where(
            (inside < rows) & (row == source * rows + inside), 1.0, 0.0
        ).astype(BF16)
        yield
        deep, broad = spread.shape
        for piece in range(x.shape[1] // deep):
            for low in range(0, broad, broad // 2):
                wide_x[:, piece * broad + low : piece * broad + low + broad // 2] = jnp.dot(
                    x[:, piece * deep : (piece + 1) * deep],
                    spread[:, low : low + broad // 2],
                    preferred_element_type=F32,
                ).astype(BF16)
                yield

    def rank_base(kind, source):
        if kind.sign > 0:
            return tbl[0, source + kind.reach + 1] - 1
        return tbl[0, source - kind.reach]

    def assemble(kind, low, high):
        base = rank_base(kind, zn)
        buf = bufs[kind.index][0]

        def one(slot, carry):
            rank = jnp.clip(base - kind.sign * slot, 0, tbl.shape[1] - 1)
            expert = jnp.clip(tbl[1, rank], 0, master.shape[0] - 1)
            if kind.part == 0:
                buf[slot] = master[expert, :head_rows, :].astype(BF16)
            else:
                buf[slot, :tail_rows, :] = master[expert, head_rows:, :lanes].astype(BF16)
                buf[slot, tail_rows:, :] = master[expert, head_rows:, lanes:].astype(BF16)
            return carry

        lax.fori_loop(low, high, one, 0)

    def extract(kind, hop):
        source = zn - kind.sign * hop
        base = rank_base(kind, source)
        buf = bufs[kind.index][hop]
        held = kind.sent(hop)
        row = lax.rem(source, n) * pad_rows
        for slot in range(SLOTS):
            index = kind.sign * (base - (tbl[0, zn] + slot))
            index = jnp.clip(index, 0, held - 1)
            if kind.part == 0:
                weights[slot, pl.ds(pl.multiple_of(row, pad_rows), head_rows), :] = buf[index]
            else:
                at = pl.ds(pl.multiple_of(row + head_rows, head_rows), tail_rows)
                weights[slot, at, :lanes] = buf[index, :tail_rows, :]
                weights[slot, at, lanes:] = buf[index, tail_rows:, :]

    most = -(-max(caps) // GROUP)

    def bundle(kind, hop, piece):
        low, high = kind.pieces(hop)[piece]
        index = (kind.index * half + hop - 1) * most + piece
        return pltpu.make_async_remote_copy(
            src_ref=bufs[kind.index][hop - 1].at[pl.ds(low, high - low)],
            dst_ref=bufs[kind.index][hop].at[pl.ds(low, high - low)],
            send_sem=send_sem.at[index],
            recv_sem=recv_sem.at[index],
            device_id={"fsdp": z_to[kind.sign]},
            device_id_type=MESH,
        )

    loads[0].wait()
    weights[...] = jnp.zeros_like(weights)
    recent = {1: [], -1: []}
    side = [attention()]
    wider = [widen()]

    def ahead(queue):
        if queue:
            try:
                next(queue[0])
            except StopIteration:
                queue.pop()

    for hop in range(1, half + 2):
        for part in range(2):
            pair = [kind for kind in kinds if kind.part == part]
            ticks = max(max(len(k.pieces(hop)), len(k.pieces(hop - 1))) for k in pair)
            for piece in range(ticks):
                for kind in pair:
                    if piece < len(kind.pieces(hop - 1)):
                        bundle(kind, hop - 1, piece).wait_recv()
                    if piece < len(kind.pieces(hop)):
                        if hop == 1:
                            assemble(kind, *kind.pieces(1)[piece])
                            queue = recent[kind.sign]
                            if len(queue) >= 2:
                                queue.pop(0).wait_send()
                            copy = bundle(kind, hop, piece)
                            copy.start()
                            queue.append(copy)
                        else:
                            copy = bundle(kind, hop, piece)
                            copy.start()
                            open_sends.append(copy)
                if hop > 1 or part + piece > 0:
                    ahead(side)
                ahead(wider)
            for kind in pair:
                if 2 <= hop <= kind.reach + 1:
                    extract(kind, hop - 1)
    for source in wider + side:
        for _ in source:
            pass

    def partial(slot, target):
        at = pl.ds(pl.multiple_of(target * share, share), share)
        return jnp.dot(wide_x[at, :], weights[slot], preferred_element_type=F32)

    def rs_copy(index, sign):
        return pltpu.make_async_remote_copy(
            src_ref=rs_out.at[index],
            dst_ref=rs_in.at[index],
            send_sem=rs_send.at[index],
            recv_sem=rs_recv.at[index],
            device_id={"rep": y_to[sign]},
            device_id_type=MESH,
        )

    def send_sum(index, sign, value):
        rs_out[index] = value.astype(BF16)
        copy = rs_copy(index, sign)
        copy.start()
        open_sends.append(copy)

    send_sum(0, 1, partial(0, y_far))
    send_sum(1, -1, partial(1, y_far))
    send_sum(2, 1, partial(1, y_to[1]))
    send_sum(3, -1, partial(0, y_to[-1]))
    up = partial(0, y_to[1])
    rs_copy(0, 1).wait_recv()
    send_sum(4, 1, up + rs_in[0].astype(F32))
    down = partial(1, y_to[-1])
    rs_copy(1, -1).wait_recv()
    send_sum(5, -1, down + rs_in[1].astype(F32))
    own = (partial(0, y), partial(1, y))
    for slot, (index, late, sign) in enumerate(((3, 4, -1), (2, 5, 1))):
        rs_copy(index, sign).wait_recv()
        rs_copy(late, -sign).wait_recv()
        value = own[slot] + rs_in[index].astype(F32) + rs_in[late].astype(F32)
        value = value / (1.0 + jnp.exp(-value))
        for side_of in range(2):
            at = slice(side_of * lanes, (side_of + 1) * lanes)
            eh_out[slot, :, at] = (value[:, at] * gate[slot]).astype(BF16)
    for copy in head_copies + open_sends + recent[1] + recent[-1]:
        copy.wait_send()


def exchange(sizes, caps, collective_id, operands):
    n, heads, reps = sizes
    tbl, lens, master, x, gate, att, qn, qr, cache, new = operands
    experts, rows, units = master.shape
    head_rows = rows * 4 // 7
    pad_rows = 1 << (rows - 1).bit_length()
    kinds = kinds_of(n, caps)
    most = -(-max(caps) // GROUP)
    copies = 4 * (n // 2) * most
    lat = cache.shape[1] - qr.shape[1]
    hdim = att.shape[2]
    total_rows = qr.shape[0]
    local_heads = qn.shape[1] // hdim
    share = x.shape[0] // reps
    group = n
    while group % 2 == 0 and group * rows // 2 % 128 == 0:
        group //= 2
    vmem = pl.BlockSpec(memory_space=pltpu.VMEM)
    smem = pl.BlockSpec(memory_space=pltpu.SMEM)
    hbm = pl.BlockSpec(memory_space=pl.ANY)
    shapes = []
    for kind in kinds:
        block = (head_rows, units) if kind.part == 0 else (2 * (rows - head_rows), units // 2)
        shapes += [(kind.sent(max(hop, 1)), *block) for hop in range(kind.reach + 1)]
    dma = pltpu.SemaphoreType.DMA
    return pl.pallas_call(
        functools.partial(body, n, heads, reps, caps),
        out_shape=(
            jax.ShapeDtypeStruct((SLOTS, share, units), BF16),
            jax.ShapeDtypeStruct(qn.shape, BF16),
        ),
        in_specs=[smem, smem, hbm, hbm, vmem, vmem, vmem, vmem, hbm, vmem],
        out_specs=(vmem, vmem),
        scratch_shapes=[pltpu.VMEM(shape, BF16) for shape in shapes]
        + [
            pltpu.VMEM(master.shape, F32),
            pltpu.VMEM(x.shape, BF16),
            pltpu.VMEM(cache.shape, BF16),
            pltpu.VMEM((x.shape[0], n * pad_rows), BF16),
            pltpu.VMEM((group * rows, group * pad_rows), BF16),
            pltpu.VMEM((SLOTS, n * pad_rows, units), BF16),
            pltpu.VMEM(att.shape, F32),
            pltpu.VMEM((local_heads, lat, 2 * hdim), BF16),
            pltpu.VMEM((total_rows, lat), BF16),
            pltpu.VMEM((total_rows, cache.shape[2]), F32),
            pltpu.VMEM((total_rows, lat), F32),
            pltpu.VMEM((6, share, units), BF16),
            pltpu.VMEM((6, share, units), BF16),
            dma((copies,)),
            dma((copies,)),
            dma((heads,)),
            dma((heads,)),
            dma((n,)),
            dma((n,)),
            dma((4,)),
            dma((4,)),
            dma((6,)),
            dma((6,)),
            dma((3,)),
        ],
        compiler_params=pltpu.CompilerParams(
            collective_id=collective_id,
            has_side_effects=True,
            vmem_limit_bytes=50 * 1024 * 1024,
        ),
    )(*operands)


def local(
    sizes,
    expert_master,
    placement,
    hidden_rows,
    routes,
    route_weight,
    att_master,
    query_nope,
    query_rope,
    cache_latent,
    cache_len,
    new_latent,
):
    n, heads, reps = sizes
    z, y = lax.axis_index("fsdp"), lax.axis_index("rep")
    count = placement.shape[0]
    ids = jnp.arange(count, dtype=jnp.int32)
    width = max(3 * n + 1, 3 * count)
    turns = jnp.arange(3, dtype=jnp.int32) * n
    places = jnp.arange(width, dtype=jnp.int32)
    below = jnp.sum(
        ((placement[None, None, :] + turns[None, :, None]) < places[:, None, None]).astype(jnp.int32),
        axis=(1, 2),
    )
    before = (placement[None, :] < placement[:, None]) | (
        (placement[None, :] == placement[:, None]) & (ids[None, :] < ids[:, None])
    )
    rank = jnp.sum(before.astype(jnp.int32), axis=1)
    ordered = jnp.sum(jnp.where(rank[None, :] == places[:, None] % count, ids[None, :], 0), axis=1)
    tbl = jnp.stack([below, ordered])
    slot_of = jnp.sum(
        ((placement[:, None] == placement[None, :]) & (ids[None, :] < ids[:, None])).astype(jnp.int32), axis=1
    )
    slots = jnp.arange(SLOTS, dtype=jnp.int32)
    here = (placement == z)[None, :] & (slot_of[None, :] == slots[:, None])
    mine = jnp.sum(jnp.where(here, ids[None, :] + 1, 0), axis=1) - 1
    share = hidden_rows.shape[0] // reps
    my_routes = lax.dynamic_slice_in_dim(routes, y * share, share, 0)
    my_weight = lax.dynamic_slice_in_dim(route_weight, y * share, share, 0)
    gate = jnp.sum(jnp.where(my_routes[None] == mine[:, None, None], my_weight[None], 0.0), axis=2)
    units = expert_master.shape[2]
    gate = jnp.broadcast_to(gate[:, :, None], (SLOTS, share, units // 2))

    lat_rows, all_heads, both = att_master.shape
    local_heads = all_heads // heads
    att = att_master.reshape(lat_rows, heads, reps, 2, 2, both // 2)
    att = lax.dynamic_index_in_dim(att, y, 2, keepdims=False)
    att = att.transpose(1, 2, 0, 3, 4).reshape(heads, lat_rows * 4, both // 2)

    steps, rows_here = query_nope.shape[0], query_nope.shape[1]
    group = steps * rows_here
    qn = query_nope.reshape(group, -1)
    qr = query_rope.reshape(group, local_heads, -1).transpose(1, 0, 2).reshape(group * local_heads, -1)
    new = new_latent.reshape(group, -1)
    operands = (tbl, cache_len, expert_master, hidden_rows, gate, att, qn, qr, jnp.swapaxes(cache_latent, 1, 2), new)

    table = [capacities(n, spread) for spread in SPREADS]
    runs = jnp.arange(1, n // 2 + 1, dtype=jnp.int32)
    away = (placement[None, :] - jnp.arange(n, dtype=jnp.int32)[:, None] + n) % n
    held = jnp.sum((away[None] < runs[:, None, None]).astype(jnp.int32), axis=2)
    fullest = jnp.max(held, axis=1)
    tier = jnp.int32(0)
    for caps in table[:-1]:
        over = jnp.any(fullest > jnp.asarray(caps[1:], jnp.int32))
        tier = jnp.where(over & (tier == table.index(caps)), tier + 1, tier)
    branches = [functools.partial(exchange, sizes, caps, index) for index, caps in enumerate(table)]
    hidden, attended = lax.switch(tier, branches, operands)
    return hidden, attended.reshape(steps, rows_here, -1)


def solution(mesh):
    placed = (
        P(None, ("rep", "fsdp"), "head"),
        P(),
        P(None, "rep"),
        P(),
        P(),
        P(("fsdp", "head"), None, None),
        P(None, ("fsdp", "rep"), "head", None),
        P(None, ("fsdp", "rep"), "head", None),
        P(("fsdp", "rep"), None, None),
        P(("fsdp", "rep")),
        P(None, ("fsdp", "rep"), None),
    )
    sizes = (mesh.shape["fsdp"], mesh.shape["head"], mesh.shape["rep"])
    return jax.shard_map(
        functools.partial(local, sizes),
        mesh=mesh,
        in_specs=placed,
        out_specs=(P("fsdp", "rep", "head"), P(None, ("fsdp", "rep"), "head")),
        check_vma=False,
    )
```

```python
import functools
import math

import jax
import jax.numpy as jnp
from jax import lax
from jax.experimental import pallas as pl
from jax.experimental.pallas import tpu as pltpu
from jax.sharding import PartitionSpec as P

MESH = pl.DeviceIdType.MESH
SLOTS = 2
GROUP = 8
F32 = jnp.float32
BF16 = jnp.bfloat16
SPREADS = (2.6, 3.8)


def capacities(n, spread):
    caps = [0]
    for length in range(1, n // 2 + 1):
        cap = 2 * length
        if spread is not None:
            drift = math.sqrt(2 * length * 0.25 * (2 * n - 2 * length) / (2 * n - 1))
            cap = min(cap, int(length + spread * drift))
        caps.append(max(cap, caps[-1], 2))
    return tuple(caps)


class Kind:
    def __init__(self, index, sign, part, reach, caps):
        self.index, self.sign, self.part, self.reach, self.caps = index, sign, part, reach, caps

    def sent(self, hop):
        return self.caps[self.reach - hop + 1]

    def pieces(self, hop):
        if hop < 1 or hop > self.reach:
            return []
        top = self.sent(hop)
        return [(low, min(low + GROUP, top)) for low in range(0, top, GROUP)]


def kinds_of(n, caps):
    half = n // 2
    return (
        Kind(0, 1, 0, half, caps),
        Kind(1, -1, 0, half - 1, caps),
        Kind(2, 1, 1, half - 1, caps),
        Kind(3, -1, 1, half, caps),
    )


def body(
    n,
    heads,
    reps,
    caps,
    tbl,
    lens,
    master_hbm,
    x_hbm,
    routes,
    route_weight,
    att,
    qn,
    qr,
    cache_hbm,
    new,
    eh_out,
    at_out,
    *refs,
):
    z, h, y = lax.axis_index("fsdp"), lax.axis_index("head"), lax.axis_index("rep")
    kinds = kinds_of(n, caps)
    bufs = []
    for kind in kinds:
        bufs.append(refs[: kind.reach + 1])
        refs = refs[kind.reach + 1 :]
    (
        master,
        x,
        cache,
        wide_x,
        spread,
        weights,
        landed,
        gate,
        total,
        maps,
        qlat,
        probs,
        latent,
        rs_out,
        rs_in,
        send_sem,
        recv_sem,
        head_send,
        head_recv,
        map_send,
        map_recv,
        y_send,
        y_recv,
        rs_send,
        rs_recv,
        load_sem,
    ) = refs
    half = n // 2
    zn = z + n
    rows = master.shape[1]
    units = master.shape[2]
    lanes = units // 2
    head_rows = rows * 4 // 7
    tail_rows = rows - head_rows
    pad_rows = wide_x.shape[1] // n
    share = x.shape[0] // reps
    local_heads, lat = maps.shape[0], maps.shape[1]
    hdim = maps.shape[2] // 2
    block = lat // n
    z_to = {1: lax.rem(z + 1, n), -1: lax.rem(z + n - 1, n)}
    y_to = {1: lax.rem(y + 1, reps), -1: lax.rem(y + reps - 1, reps)}
    y_far = lax.rem(y + 2, reps)

    loads = [
        pltpu.make_async_copy(master_hbm, master, load_sem.at[0]),
        pltpu.make_async_copy(x_hbm, x, load_sem.at[1]),
        pltpu.make_async_copy(cache_hbm, cache, load_sem.at[2]),
    ]
    for load in loads:
        load.start()

    barrier = pltpu.get_barrier_semaphore()
    for sign in (1, -1):
        pl.semaphore_signal(barrier, inc=1, device_id={"fsdp": z_to[sign]}, device_id_type=MESH)
        pl.semaphore_signal(barrier, inc=1, device_id={"rep": y_to[sign]}, device_id_type=MESH)
    for step in range(1, heads):
        pl.semaphore_signal(
            barrier, inc=1, device_id={"head": lax.rem(h + step, heads)}, device_id_type=MESH
        )
    pl.semaphore_wait(barrier, 4 + heads - 1)

    head_copies = []
    for step in range(1, heads):
        to = lax.rem(h + step, heads)
        copy = pltpu.make_async_remote_copy(
            src_ref=att.at[:, pl.ds(pl.multiple_of(to * local_heads, local_heads), local_heads), :],
            dst_ref=landed.at[h],
            send_sem=head_send.at[step],
            recv_sem=head_recv.at[h],
            device_id={"head": to},
            device_id_type=MESH,
        )
        copy.start()
        head_copies.append(copy)

    def head_arrival(step):
        source = lax.rem(h + step, heads)
        return pltpu.make_async_remote_copy(
            src_ref=landed.at[h],
            dst_ref=landed.at[source],
            send_sem=head_send.at[step],
            recv_sem=head_recv.at[source],
            device_id={"head": source},
            device_id_type=MESH,
        )

    def map_block(sign, hop):
        owner = lax.rem(zn - sign * hop, n)
        return maps.at[pl.ds(2 * y, 2), pl.ds(pl.multiple_of(owner * block, block), block), :]

    def map_copy(sign, hop):
        index = half * (sign < 0) + hop - 1
        ref = map_block(sign, hop - 1)
        return pltpu.make_async_remote_copy(
            src_ref=ref,
            dst_ref=ref,
            send_sem=map_send.at[index],
            recv_sem=map_recv.at[index],
            device_id={"fsdp": z_to[sign]},
            device_id_type=MESH,
        )

    def map_arrival(sign, hop):
        index = half * (sign < 0) + hop - 1
        ref = map_block(sign, hop)
        return pltpu.make_async_remote_copy(
            src_ref=ref,
            dst_ref=ref,
            send_sem=map_send.at[index],
            recv_sem=map_recv.at[index],
            device_id={"fsdp": z_to[sign]},
            device_id_type=MESH,
        )

    def y_copy(index, sign, low, size):
        ref = maps.at[pl.ds(low, size)]
        return pltpu.make_async_remote_copy(
            src_ref=ref,
            dst_ref=ref,
            send_sem=y_send.at[index],
            recv_sem=y_recv.at[index],
            device_id={"rep": y_to[sign]},
            device_id_type=MESH,
        )

    open_sends = []

    def attention():
        for step in range(1, heads):
            head_arrival(step).wait_recv()
        landed[h] = att[:, pl.ds(pl.multiple_of(h * local_heads, local_heads), local_heads), :]
        per = att.shape[0] * local_heads
        flat = landed[...].reshape(heads * per, 2 * hdim).astype(BF16)
        row = lax.broadcasted_iota(jnp.int32, (block, heads * per), 0)
        col = lax.broadcasted_iota(jnp.int32, (block, heads * per), 1)
        for hq in range(2):
            want = (row >> 1) * per + (row & 1) * local_heads + 2 * y + hq
            pick = jnp.where(col == want, 1.0, 0.0).astype(BF16)
            maps[2 * y + hq, pl.ds(pl.multiple_of(z * block, block), block), :] = jnp.dot(
                pick, flat, preferred_element_type=F32
            ).astype(BF16)
        for hop in range(1, half + 2):
            for sign in (1, -1):
                top = half if sign > 0 else half - 1
                if 2 <= hop <= top + 1:
                    map_arrival(sign, hop - 1).wait_recv()
                if hop <= top:
                    copy = map_copy(sign, hop)
                    copy.start()
                    open_sends.append(copy)
            yield
        first = [y_copy(0, 1, 2 * y, 2), y_copy(1, -1, 2 * y, 2)]
        for copy in first:
            copy.start()
            open_sends.append(copy)
        for _ in range(5):
            yield
        y_copy(0, 1, 2 * y_to[-1], 2).wait_recv()
        y_copy(1, -1, 2 * y_to[1], 2).wait_recv()
        second = [y_copy(2, 1, 2 * y_to[-1], 1), y_copy(3, -1, 2 * y_to[1] + 1, 1)]
        for copy in second:
            copy.start()
            open_sends.append(copy)
        for _ in range(3):
            yield
        y_copy(2, 1, 2 * y_far, 1).wait_recv()
        y_copy(3, -1, 2 * y_far + 1, 1).wait_recv()
        loads[2].wait()
        yield
        total_rows = qn.shape[0]
        group = total_rows // local_heads
        order = lax.broadcasted_iota(jnp.int32, (total_rows, total_rows), 0)
        order = (order & (group - 1)) * local_heads + (order >> (group.bit_length() - 1))
        spot = lax.broadcasted_iota(jnp.int32, (total_rows, total_rows), 1)
        pick = jnp.where(order == spot, 1.0, 0.0).astype(BF16)
        q_all = jnp.dot(pick, qn[...], preferred_element_type=F32).astype(BF16)
        q_rope = jnp.dot(pick, qr[...], preferred_element_type=F32).astype(BF16)
        contract = (((1,), (1,)), ((), ()))
        for head in range(local_heads):
            q = q_all[head * group : (head + 1) * group]
            qlat[head * group : (head + 1) * group, :] = lax.dot_general(
                q, maps[head, :, :hdim], contract, preferred_element_type=F32
            ).astype(BF16)
        yield
        count, slots = cache.shape[0], cache.shape[2]
        scale = 1.0 / math.sqrt(hdim + qr.shape[1])
        row = lax.broadcasted_iota(jnp.int32, (total_rows, slots), 0) & (count - 1)
        col = lax.broadcasted_iota(jnp.int32, (total_rows, slots), 1)
        probs[...] = jnp.full((total_rows, slots), -1e30, F32)
        for r in range(count):
            part = jnp.dot(qlat[...], cache[r, :lat, :], preferred_element_type=F32) + jnp.dot(
                q_rope, cache[r, lat:, :], preferred_element_type=F32
            )
            probs[...] = jnp.where((row == r) & (col < lens[r]), part * scale, probs[...])
            yield
        fresh = lax.dot_general(
            qlat[...], new[:, :lat], contract, preferred_element_type=F32
        ) + lax.dot_general(q_rope, new[:, lat:], contract, preferred_element_type=F32)
        nrow = lax.broadcasted_iota(jnp.int32, fresh.shape, 0)
        ncol = lax.broadcasted_iota(jnp.int32, fresh.shape, 1)
        shift = count.bit_length() - 1
        same = (nrow & (count - 1)) == (ncol & (count - 1))
        step_of = (nrow >> shift) & (group // count - 1)
        fresh = jnp.where(same & ((ncol >> shift) <= step_of), fresh * scale, -1e30)
        score = probs[...]
        top = jnp.maximum(
            jnp.max(score, axis=1, keepdims=True), jnp.max(fresh, axis=1, keepdims=True)
        )
        old_exp = jnp.exp(score - top)
        new_exp = jnp.exp(fresh - top)
        mass = jnp.sum(old_exp, axis=1, keepdims=True) + jnp.sum(new_exp, axis=1, keepdims=True)
        probs[...] = old_exp / mass
        new_probs = (new_exp / mass).astype(BF16)
        latent[...] = jnp.dot(new_probs, new[:, :lat], preferred_element_type=F32)
        yield
        for r in range(count):
            mine = jnp.where(row == r, probs[...], 0.0).astype(BF16)
            latent[...] += lax.dot_general(
                mine, cache[r, :lat, :], contract, preferred_element_type=F32
            )
            yield
        for head in range(local_heads):
            lh = latent[head * group : (head + 1) * group, :].astype(BF16)
            at_out[:, head * hdim : (head + 1) * hdim] = jnp.dot(
                lh, maps[head, :, hdim:], preferred_element_type=F32
            ).astype(BF16)

    def widen():
        weights[...] = jnp.zeros_like(weights)
        for slot in range(SLOTS):
            rank = jnp.clip(tbl[0, zn] + slot, 0, tbl.shape[1] - 1)
            expert = jnp.clip(tbl[1, rank], 0, master.shape[0] - 1)
            weights[slot, pl.ds(pl.multiple_of(z * pad_rows, pad_rows), rows), :] = master[
                expert
            ].astype(BF16)
            live = tbl[0, zn] + slot < tbl[0, zn + 1]
            at = pl.ds(pl.multiple_of(y * share, share), share)
            hit = jnp.where(routes[:, at] == jnp.where(live, expert, -1), route_weight[:, at], 0.0)
            gate[slot] = jnp.broadcast_to(jnp.sum(hit, axis=0, keepdims=True), (lanes, share)).T
        loads[1].wait()
        yield
        row = lax.broadcasted_iota(jnp.int32, spread.shape, 0)
        col = lax.broadcasted_iota(jnp.int32, spread.shape, 1)
        inside = col & (pad_rows - 1)
        source = col >> (pad_rows.bit_length() - 1)
        spread[...] = jnp.where(
            (inside < rows) & (row == source * rows + inside), 1.0, 0.0
        ).astype(BF16)
        yield
        deep, broad = spread.shape
        for piece in range(x.shape[1] // deep):
            for low in range(0, broad, broad // 2):
                wide_x[:, piece * broad + low : piece * broad + low + broad // 2] = jnp.dot(
                    x[:, piece * deep : (piece + 1) * deep],
                    spread[:, low : low + broad // 2],
                    preferred_element_type=F32,
                ).astype(BF16)
                yield

    def rank_base(kind, source):
        if kind.sign > 0:
            return tbl[0, source + kind.reach + 1] - 1
        return tbl[0, source - kind.reach]

    def assemble(kind, low, high):
        base = rank_base(kind, zn)
        buf = bufs[kind.index][0]

        def one(slot, carry):
            rank = jnp.clip(base - kind.sign * slot, 0, tbl.shape[1] - 1)
            expert = jnp.clip(tbl[1, rank], 0, master.shape[0] - 1)
            if kind.part == 0:
                buf[slot] = master[expert, :head_rows, :].astype(BF16)
            else:
                buf[slot, :tail_rows, :] = master[expert, head_rows:, :lanes].astype(BF16)
                buf[slot, tail_rows:, :] = master[expert, head_rows:, lanes:].astype(BF16)
            return carry

        lax.fori_loop(low, high, one, 0)

    def extract(kind, hop):
        source = zn - kind.sign * hop
        base = rank_base(kind, source)
        buf = bufs[kind.index][hop]
        held = kind.sent(hop)
        row = lax.rem(source, n) * pad_rows
        for slot in range(SLOTS):
            index = kind.sign * (base - (tbl[0, zn] + slot))
            index = jnp.clip(index, 0, held - 1)
            if kind.part == 0:
                weights[slot, pl.ds(pl.multiple_of(row, pad_rows), head_rows), :] = buf[index]
            else:
                at = pl.ds(pl.multiple_of(row + head_rows, head_rows), tail_rows)
                weights[slot, at, :lanes] = buf[index, :tail_rows, :]
                weights[slot, at, lanes:] = buf[index, tail_rows:, :]

    most = -(-max(caps) // GROUP)

    def bundle(kind, hop, piece):
        low, high = kind.pieces(hop)[piece]
        index = (kind.index * half + hop - 1) * most + piece
        return pltpu.make_async_remote_copy(
            src_ref=bufs[kind.index][hop - 1].at[pl.ds(low, high - low)],
            dst_ref=bufs[kind.index][hop].at[pl.ds(low, high - low)],
            send_sem=send_sem.at[index],
            recv_sem=recv_sem.at[index],
            device_id={"fsdp": z_to[kind.sign]},
            device_id_type=MESH,
        )

    loads[0].wait()
    recent = {1: [], -1: []}
    side = [attention()]
    wider = [widen()]

    def ahead(queue):
        if queue:
            try:
                next(queue[0])
            except StopIteration:
                queue.pop()

    for hop in range(1, half + 2):
        for part in range(2):
            pair = [kind for kind in kinds if kind.part == part]
            ticks = max(max(len(k.pieces(hop)), len(k.pieces(hop - 1))) for k in pair)
            for piece in range(ticks):
                for kind in pair:
                    if piece < len(kind.pieces(hop - 1)):
                        bundle(kind, hop - 1, piece).wait_recv()
                    if piece < len(kind.pieces(hop)):
                        if hop == 1:
                            assemble(kind, *kind.pieces(1)[piece])
                            queue = recent[kind.sign]
                            if len(queue) >= 2:
                                queue.pop(0).wait_send()
                            copy = bundle(kind, hop, piece)
                            copy.start()
                            queue.append(copy)
                        else:
                            copy = bundle(kind, hop, piece)
                            copy.start()
                            open_sends.append(copy)
                if hop > 1 or part + piece > 0:
                    ahead(side)
                ahead(wider)
            for kind in pair:
                if 2 <= hop <= kind.reach + 1:
                    extract(kind, hop - 1)
    for source in wider + side:
        for _ in source:
            pass

    def partial(slot, target):
        at = pl.ds(pl.multiple_of(target * share, share), share)
        return total[slot, at, :]

    def rs_copy(index, sign):
        return pltpu.make_async_remote_copy(
            src_ref=rs_out.at[index],
            dst_ref=rs_in.at[index],
            send_sem=rs_send.at[index],
            recv_sem=rs_recv.at[index],
            device_id={"rep": y_to[sign]},
            device_id_type=MESH,
        )

    def send_sum(index, sign, value):
        rs_out[index] = value.astype(BF16)
        copy = rs_copy(index, sign)
        copy.start()
        open_sends.append(copy)

    def multiply(slot, carry):
        total[slot] = jnp.dot(wide_x[...], weights[slot], preferred_element_type=F32)
        return carry

    lax.fori_loop(0, SLOTS, multiply, 0)
    send_sum(0, 1, partial(0, y_far))
    send_sum(1, -1, partial(1, y_far))
    send_sum(2, 1, partial(1, y_to[1]))
    send_sum(3, -1, partial(0, y_to[-1]))
    up = partial(0, y_to[1])
    rs_copy(0, 1).wait_recv()
    send_sum(4, 1, up + rs_in[0].astype(F32))
    down = partial(1, y_to[-1])
    rs_copy(1, -1).wait_recv()
    send_sum(5, -1, down + rs_in[1].astype(F32))
    own = (partial(0, y), partial(1, y))
    for slot, (index, late, sign) in enumerate(((3, 4, -1), (2, 5, 1))):
        rs_copy(index, sign).wait_recv()
        rs_copy(late, -sign).wait_recv()
        value = own[slot] + rs_in[index].astype(F32) + rs_in[late].astype(F32)
        value = value / (1.0 + jnp.exp(-value))
        for side_of in range(2):
            at = slice(side_of * lanes, (side_of + 1) * lanes)
            eh_out[slot, :, at] = (value[:, at] * gate[slot]).astype(BF16)
    for copy in head_copies + open_sends + recent[1] + recent[-1]:
        copy.wait_send()


def exchange(sizes, caps, collective_id, operands):
    n, heads, reps = sizes
    tbl, lens, master, x, routes, route_weight, att, qn, qr, cache, new = operands
    experts, rows, units = master.shape
    head_rows = rows * 4 // 7
    pad_rows = 1 << (rows - 1).bit_length()
    kinds = kinds_of(n, caps)
    most = -(-max(caps) // GROUP)
    copies = 4 * (n // 2) * most
    lat = cache.shape[1] - qr.shape[1]
    hdim = att.shape[2] // 2
    total_rows = qr.shape[0]
    local_heads = att.shape[1] // heads
    share = x.shape[0] // reps
    group = n
    while group % 2 == 0 and group * rows // 2 % 128 == 0:
        group //= 2
    vmem = pl.BlockSpec(memory_space=pltpu.VMEM)
    smem = pl.BlockSpec(memory_space=pltpu.SMEM)
    hbm = pl.BlockSpec(memory_space=pl.ANY)
    shapes = []
    for kind in kinds:
        block = (head_rows, units) if kind.part == 0 else (2 * (rows - head_rows), units // 2)
        shapes += [(kind.sent(max(hop, 1)), *block) for hop in range(kind.reach + 1)]
    dma = pltpu.SemaphoreType.DMA
    return pl.pallas_call(
        functools.partial(body, n, heads, reps, caps),
        out_shape=(
            jax.ShapeDtypeStruct((SLOTS, share, units), BF16),
            jax.ShapeDtypeStruct((total_rows // local_heads, local_heads * hdim), BF16),
        ),
        in_specs=[smem, smem, hbm, hbm, vmem, vmem, vmem, vmem, vmem, hbm, vmem],
        out_specs=(vmem, vmem),
        scratch_shapes=[pltpu.VMEM(shape, BF16) for shape in shapes]
        + [
            pltpu.VMEM(master.shape, F32),
            pltpu.VMEM(x.shape, BF16),
            pltpu.VMEM(cache.shape, BF16),
            pltpu.VMEM((x.shape[0], n * pad_rows), BF16),
            pltpu.VMEM((group * rows, group * pad_rows), BF16),
            pltpu.VMEM((SLOTS, n * pad_rows, units), BF16),
            pltpu.VMEM((heads, att.shape[0], local_heads, 2 * hdim), F32),
            pltpu.VMEM((SLOTS, share, units // 2), F32),
            pltpu.VMEM((SLOTS, x.shape[0], units), F32),
            pltpu.VMEM((local_heads, lat, 2 * hdim), BF16),
            pltpu.VMEM((total_rows, lat), BF16),
            pltpu.VMEM((total_rows, cache.shape[2]), F32),
            pltpu.VMEM((total_rows, lat), F32),
            pltpu.VMEM((6, share, units), BF16),
            pltpu.VMEM((6, share, units), BF16),
            dma((copies,)),
            dma((copies,)),
            dma((heads,)),
            dma((heads,)),
            dma((n,)),
            dma((n,)),
            dma((4,)),
            dma((4,)),
            dma((6,)),
            dma((6,)),
            dma((3,)),
        ],
        compiler_params=pltpu.CompilerParams(
            collective_id=collective_id,
            has_side_effects=True,
            vmem_limit_bytes=50 * 1024 * 1024,
        ),
    )(*operands)


def plain(
    expert_master,
    placement,
    hidden_rows,
    routes,
    route_weight,
    att_master,
    query_nope,
    query_rope,
    cache_latent,
    cache_len,
    new_latent,
):
    owners = lax.axis_size("fsdp")
    hdim = query_nope.shape[3]
    query_lat = cache_latent.shape[2] - query_rope.shape[3]
    count = placement.shape[0]
    expert_ids = jnp.arange(count, dtype=jnp.int32)
    same = placement[:, None] == placement[None, :]
    earlier = expert_ids[None, :] < expert_ids[:, None]
    slot_of = jnp.sum((same & earlier).astype(jnp.int32), axis=1)
    owner_ids = jnp.arange(owners, dtype=jnp.int32)
    slot_ids = jnp.arange(SLOTS, dtype=jnp.int32)
    match = (slot_ids[:, None, None] == slot_of[None, None, :]) & (
        owner_ids[None, :, None] == placement[None, None, :]
    )
    picked = jnp.sum(jnp.where(match, expert_ids[None, None, :], 0), axis=2)
    filled = jnp.any(match, axis=2)
    row_count = expert_master.shape[1]
    unit_count = expert_master.shape[2]
    mine = lax.axis_index("fsdp")
    share_rows = hidden_rows.shape[0] // lax.axis_size("rep")
    first_row = lax.axis_index("rep") * share_rows
    blocks = jnp.take(expert_master, picked.reshape(-1), axis=0).astype(jnp.bfloat16)
    blocks = blocks.reshape(SLOTS, owners, row_count, unit_count)
    outgoing = jnp.where(filled[:, :, None, None], blocks, jnp.zeros_like(blocks))
    arrived = lax.all_to_all(outgoing, "fsdp", split_axis=1, concat_axis=1, tiled=True)
    weights_here = arrived.reshape(SLOTS, owners * row_count, unit_count)
    my_experts = lax.dynamic_index_in_dim(picked, mine, 1, keepdims=False)
    my_filled = lax.dynamic_index_in_dim(filled, mine, 1, keepdims=False)
    terms = jnp.einsum("rd,sdf->srf", hidden_rows, weights_here, preferred_element_type=jnp.float32)
    hits = routes[None, :, :] == my_experts[:, None, None]
    gate = jnp.sum(jnp.where(hits, route_weight[None, :, :], 0.0), axis=2)
    gate = jnp.where(my_filled[:, None], gate, 0.0)
    shares = lax.all_to_all(terms, "rep", split_axis=1, concat_axis=0, tiled=True)
    share = jnp.sum(shares.reshape(-1, SLOTS, share_rows, unit_count), axis=0)
    gate_share = lax.dynamic_slice_in_dim(gate, first_row, share_rows, 1)
    activated = (jax.nn.silu(share) * gate_share[:, :, None]).astype(jnp.bfloat16)
    local_maps = att_master.astype(jnp.bfloat16)[None]
    copies = jnp.broadcast_to(local_maps, (owners, *local_maps.shape[1:]))
    widened = lax.all_to_all(copies, "fsdp", split_axis=0, concat_axis=0, tiled=True)
    spread = lax.all_to_all(widened[:, None], "head", split_axis=3, concat_axis=1, tiled=True)
    maps = spread.reshape(-1, spread.shape[3], spread.shape[4])
    key_map = maps[:, :, :hdim]
    value_map = maps[:, :, hdim:]
    q_latent = jnp.einsum(
        "trhd,lhd->trhl", query_nope, key_map, preferred_element_type=jnp.float32
    ).astype(jnp.bfloat16)
    query_full = jnp.concatenate([q_latent, query_rope], axis=3)
    scale = 1.0 / math.sqrt(query_nope.shape[3] + query_rope.shape[3])
    old_scores = (
        jnp.einsum("trhc,rjc->trhj", query_full, cache_latent, preferred_element_type=jnp.float32)
        * scale
    )
    new_scores = (
        jnp.einsum("trhc,urc->trhu", query_full, new_latent, preferred_element_type=jnp.float32)
        * scale
    )
    positions = jnp.arange(cache_latent.shape[1], dtype=jnp.int32)
    live = positions[None, :] < cache_len[:, None]
    old_scores = jnp.where(live[None, :, None, :], old_scores, -1e30)
    step_ids = jnp.arange(new_latent.shape[0], dtype=jnp.int32)
    causal = step_ids[None, :] <= step_ids[:, None]
    new_scores = jnp.where(causal[:, None, None, :], new_scores, -1e30)
    highest = jnp.maximum(jnp.max(old_scores, axis=3), jnp.max(new_scores, axis=3))
    old_exp = jnp.exp(old_scores - highest[..., None])
    new_exp = jnp.exp(new_scores - highest[..., None])
    total = jnp.sum(old_exp, axis=3) + jnp.sum(new_exp, axis=3)
    old_probs = (old_exp / total[..., None]).astype(jnp.bfloat16)
    new_probs = (new_exp / total[..., None]).astype(jnp.bfloat16)
    latent_full = jnp.einsum(
        "trhj,rjc->trhc", old_probs, cache_latent, preferred_element_type=jnp.float32
    )
    latent_full = latent_full + jnp.einsum(
        "trhu,urc->trhc", new_probs, new_latent, preferred_element_type=jnp.float32
    )
    latent_out = latent_full[..., :query_lat].astype(jnp.bfloat16)
    attention = jnp.einsum(
        "trhl,lhv->trhv", latent_out, value_map, preferred_element_type=jnp.float32
    ).astype(jnp.bfloat16)
    attention_out = attention.reshape(
        attention.shape[0], attention.shape[1], attention.shape[2] * attention.shape[3]
    )
    return (activated, attention_out)


def local(
    sizes,
    expert_master,
    placement,
    hidden_rows,
    routes,
    route_weight,
    att_master,
    query_nope,
    query_rope,
    cache_latent,
    cache_len,
    new_latent,
):
    n, heads, reps = sizes
    z, y = lax.axis_index("fsdp"), lax.axis_index("rep")
    count = placement.shape[0]
    ids = jnp.arange(count, dtype=jnp.int32)
    width = max(3 * n + 1, 3 * count)
    places = jnp.arange(width, dtype=jnp.int32)
    below = sum(
        jnp.sum((placement[None, :] < (places - turn * n)[:, None]).astype(jnp.int32), axis=1)
        for turn in range(3)
    )
    before = (placement[None, :] < placement[:, None]) | (
        (placement[None, :] == placement[:, None]) & (ids[None, :] < ids[:, None])
    )
    rank = jnp.sum(before.astype(jnp.int32), axis=1)
    ordered = jnp.sum(jnp.where(rank[None, :] == places[:, None] % count, ids[None, :], 0), axis=1)
    tbl = jnp.stack([below, ordered])
    local_heads = att_master.shape[1] // heads
    steps, rows_here = query_nope.shape[0], query_nope.shape[1]
    group = steps * rows_here
    operands = (
        tbl,
        cache_len,
        expert_master,
        hidden_rows,
        routes.T,
        route_weight.T,
        att_master,
        query_nope.reshape(group * local_heads, -1),
        query_rope.reshape(group * local_heads, -1),
        jnp.swapaxes(cache_latent, 1, 2),
        new_latent.reshape(group, -1),
    )

    table = [capacities(n, spread) for spread in SPREADS]
    runs = jnp.arange(1, n // 2 + 1, dtype=jnp.int32)
    away = (placement[None, :] - jnp.arange(n, dtype=jnp.int32)[:, None] + n) % n
    held = jnp.sum((away[None] < runs[:, None, None]).astype(jnp.int32), axis=2)
    fullest = jnp.max(held, axis=1)
    limits = jnp.asarray([caps[1:] for caps in table], jnp.int32)
    tier = jnp.sum(jnp.any(fullest[None, :] > limits, axis=1).astype(jnp.int32))
    branches = [functools.partial(exchange, sizes, caps, index) for index, caps in enumerate(table)]

    def otherwise(_):
        hidden, attended = plain(
            expert_master,
            placement,
            hidden_rows,
            routes,
            route_weight,
            att_master,
            query_nope,
            query_rope,
            cache_latent,
            cache_len,
            new_latent,
        )
        return hidden, attended.reshape(group, -1)

    hidden, attended = lax.switch(tier, [*branches, otherwise], operands)
    return hidden, attended.reshape(steps, rows_here, -1)


def solution(mesh):
    placed = (
        P(None, ("rep", "fsdp"), "head"),
        P(),
        P(None, "rep"),
        P(),
        P(),
        P(("fsdp", "head"), None, None),
        P(None, ("fsdp", "rep"), "head", None),
        P(None, ("fsdp", "rep"), "head", None),
        P(("fsdp", "rep"), None, None),
        P(("fsdp", "rep")),
        P(None, ("fsdp", "rep"), None),
    )
    sizes = (mesh.shape["fsdp"], mesh.shape["head"], mesh.shape["rep"])
    return jax.shard_map(
        functools.partial(local, sizes),
        mesh=mesh,
        in_specs=placed,
        out_specs=(P("fsdp", "rep", "head"), P(None, ("fsdp", "rep"), "head")),
        check_vma=False,
    )
```
